32 devices in a mesh: grp: 2 (over y), krow: 4 (over z), exc: 2 (over x), band: 2 (over core).
Axes of the slice: x: 2, y: 2, z: 4, core: 2. Of those that a mesh axis runs over, the one named last changes fastest.
Arguments:
- coef_zero: bfloat16 [800, 4, 4, 512], P(('grp', 'exc'), None, None, 'krow'), parts along dimension 0, may hold values from -6 to 6
- coef_shift: bfloat16 [4, 800, 4, 4, 512], P(None, ('grp', 'exc'), 'band', None, 'krow'), parts along dimension 1, may hold values from -6 to 6
- coupling: bfloat16 [2, 8, 9, 4, 4, 512], P(None, 'grp', None, None, None, 'krow'), parts along dimension 1, may hold values from -6 to 6
- partner: int32 [4, 512], replicated, may hold values from 0 to 511, as said below
Outputs:
- exciton_coupling: float32 [800, 4, 9, 400], P(('grp', 'krow'), 'band', None, 'exc'), parts along dimension 0
The draws below stay inside these ranges and needn't reach their ends.
There are 2 independent parts, one for each index of `grp`. The reference program is written for one: setup_inputs(seed, part) draws one part's arguments, and reference() takes and returns one part's arrays. A program takes and returns all parts, laid end to end along the dimension named above; an argument that names none is the same for every part. Nothing has to cross between parts.
Inputs may be any that keep to these rules, and one draw needn't show every extreme that they name: For every q, partner[q] is a permutation of the k points; the k points of one aligned block of 128 have their partners in exactly 4 such blocks, 32 in each.
All inputs are finite; a program needn't handle non-finite values.
Results may differ from the reference program's by a relative error of at most 0.0029.
Values may be sent and summed in bfloat16 or wider, within the bound.
A program may use at most 192 MiB of HBM per device.

```python
import jax
import jax.numpy as jnp
from jax import lax

NS = 400
MODES = 9
VALENCE = 4
CONDUCTION = 4
NQ = 4
K_DEV = 128
PEERS = 4
NK = 512
CAP = 32
LOWER = 2


def draw_partner(key, part):
    key = jax.random.fold_in(key, 7)
    blocks = NK // K_DEV

    def one(qkey):
        first, second, third = jax.random.split(qkey, 3)
        offsets = jax.random.permutation(first, blocks)[:PEERS]
        local_perm = jax.vmap(lambda kk: jax.random.permutation(kk, K_DEV))(jax.random.split(second, blocks))
        dest_perm = jax.vmap(lambda kk: jax.random.permutation(kk, K_DEV))(jax.random.split(third, blocks))
        source = jnp.arange(blocks, dtype=jnp.int32)[:, None]
        turn = local_perm // CAP
        target = (source + offsets[turn]) % blocks
        position = dest_perm[target, local_perm]
        return (target * K_DEV + position).reshape(-1).astype(jnp.int32)
    return jax.vmap(one)(jax.random.split(key, NQ))


def shard_levels(key, dims, cuts, least, top_value):
    factor_of = 1.0
    for dim, shards_of in cuts:
        draws = jax.random.uniform(jax.random.fold_in(jax.random.fold_in(key, 6), dim), (shards_of,), jnp.float32, least / len(cuts), top_value / len(cuts))
        factor_of = factor_of * jnp.repeat(jnp.exp(draws), dims[dim] // shards_of).reshape((-1,) + (1,) * (len(dims) - 1 - dim))
    return factor_of


def gaussian(stream_key, extent, deviation, bound, cuts=(), held_as=jnp.bfloat16):
    factor_of = shard_levels(stream_key, extent, cuts, -0.22, 0.18) if cuts else 1.0
    drawn = jax.random.normal(stream_key, extent, jnp.float32) * deviation * factor_of
    return jnp.minimum(jnp.maximum(drawn, -bound), bound).astype(held_as)


def setup_inputs(seed: int = 0, part: int = 0) -> dict:
    seeds = jax.random.split(jax.random.key(seed), 5)
    part_keys = jax.random.split(jax.random.fold_in(seeds[4], part), 5)
    coef_zero = gaussian(part_keys[0], (NS, VALENCE, CONDUCTION, NK), 1.0, 6.0, ((0, 2), (3, 4)))
    coef_shift = gaussian(part_keys[1], (NQ, NS, VALENCE, CONDUCTION, NK), 1.0, 6.0, ((1, 2), (2, 2), (4, 4)))
    coupling = gaussian(part_keys[2], (2, NQ, MODES, 4, 4, NK), 1.0, 6.0, ((5, 4),))
    partner = draw_partner(jax.random.fold_in(seeds[4], 71), part)
    return dict(coef_zero=coef_zero, coef_shift=coef_shift, coupling=coupling, partner=partner)


def reference(coef_zero, coef_shift, coupling, partner):
    nk = coef_zero.shape[-1]
    zero_flat = coef_zero.reshape(NS, -1)
    scale = (16.0 * nk) ** -0.5
    halves = VALENCE // LOWER
    bands = jnp.arange(VALENCE, dtype=jnp.int32) // LOWER

    def per_q(q):
        coef_q = coef_shift[q]
        shifted = jnp.take(coef_q, partner[q], axis=-1)
        elec_table = coupling[0, q].astype(jnp.float32)
        hole_table = coupling[1, q].astype(jnp.float32)

        def per_mode(m):
            elec = jnp.einsum("svak,ack->svck", shifted.astype(jnp.float32), elec_table[m])
            total = jnp.zeros((NS, NS), jnp.float32)
            for h in range(halves):
                inside = (bands == h)[None, :, None, None]
                masked = jnp.where(inside, coef_q.astype(jnp.float32), 0.0)
                hole = jnp.einsum("swck,vwk->svck", masked, hole_table[m])
                difference = (jnp.where(inside, elec, 0.0) - hole).astype(jnp.bfloat16).reshape(NS, -1)
                total = total + lax.dot_general(zero_flat, difference, (((1,), (1,)), ((), ())),
                                                preferred_element_type=jnp.float32)
            return total * scale

        return lax.map(per_mode, jnp.arange(MODES, dtype=jnp.int32))

    result = lax.map(per_q, jnp.arange(NQ, dtype=jnp.int32))
    return jnp.transpose(result, (2, 0, 1, 3))
```

```python
import functools

import jax
import jax.numpy as jnp
from jax import lax
from jax.experimental import pallas as pl
from jax.experimental.pallas import tpu as pltpu
from jax.sharding import PartitionSpec as P

PEERS = 4
ROWS = 16
LANES = 128
COLS = 384
LIMIT = 40 * 2**20


def round_up(n, unit):
    return (n + unit - 1) // unit * unit


def pick_kernel(x_ref, sel_ref, out_ref):
    nrow, width, _ = sel_ref.shape
    wide = sel_ref.shape[2]
    for d in range(nrow):
        for v in range(x_ref.shape[1] // width):
            got = jnp.dot(
                x_ref[:, v * width : (v + 1) * width], sel_ref[d], preferred_element_type=jnp.float32
            )
            out_ref[d, :, v * wide : (v + 1) * wide] = got.astype(jnp.bfloat16)


def build_table(x_ref, c_ref, table, modes, nval, ncond, elec):
    rows = x_ref.shape[0]

    def chunk(r, carry):
        at = pl.multiple_of(r * ROWS, ROWS)

        def slab(g):
            piece = x_ref[pl.ds(at, ROWS), g * LANES : (g + 1) * LANES]
            return piece.astype(jnp.float32).reshape(ROWS // 8, 8, LANES)

        for outer in range(nval if elec else ncond):
            if elec:
                slabs = [slab(outer * ncond + a) for a in range(ncond)]
            else:
                slabs = [slab(w * ncond + outer) for w in range(nval)]
            for m in range(modes):
                for inner in range(ncond if elec else nval):
                    if elec:
                        ids = [(m * ncond + a) * ncond + inner for a in range(ncond)]
                        g = outer * ncond + inner
                    else:
                        ids = [(m * nval + inner) * nval + w for w in range(nval)]
                        g = inner * ncond + outer
                    total = slabs[0] * c_ref[ids[0]][None]
                    for one, i in zip(slabs[1:], ids[1:]):
                        total = total + one * c_ref[i][None]
                    table[pl.ds(m * rows + at, ROWS), g * LANES : (g + 1) * LANES] = total.reshape(
                        ROWS, LANES
                    ).astype(jnp.bfloat16)
        return carry

    lax.fori_loop(0, rows // ROWS, chunk, 0)
    used = modes * rows
    if used < table.shape[0]:
        table[used:, :] = jnp.zeros((table.shape[0] - used, table.shape[1]), jnp.bfloat16)


def contract(z_ref, table, write):
    def cols(j, carry):
        at = pl.multiple_of(j * COLS, COLS)
        write(
            at,
            lax.dot_general(
                z_ref[...],
                table[pl.ds(at, COLS), :],
                (((1,), (1,)), ((), ())),
                preferred_element_type=jnp.float32,
            ),
        )
        return carry

    lax.fori_loop(0, table.shape[0] // COLS, cols, 0)


def hole_kernel(modes, nval, ncond, x_ref, c_ref, z_ref, out_ref, table):
    build_table(x_ref, c_ref, table, modes, nval, ncond, False)

    def write(at, got):
        out_ref[:, pl.ds(at, COLS)] = got

    contract(z_ref, table, write)


def elec_kernel(modes, nval, ncond, f_ref, inc_ref, perm_ref, c_ref, z_ref, hole_ref, out_ref, x_ref, table):
    nrow = inc_ref.shape[0]
    wide = inc_ref.shape[2] // nval
    width = perm_ref.shape[1]
    for v in range(nval):
        got = jnp.zeros((x_ref.shape[0], width), jnp.float32)
        for o in range(nrow):
            got = got + jnp.dot(
                inc_ref[o, :, v * wide : (v + 1) * wide],
                perm_ref[o * wide : (o + 1) * wide, :],
                preferred_element_type=jnp.float32,
            )
        x_ref[:, v * width : (v + 1) * width] = got.astype(jnp.bfloat16)
    build_table(x_ref, c_ref, table, modes, nval, ncond, True)
    factor = f_ref[0]

    def write(at, got):
        out_ref[:, pl.ds(at, COLS)] = (got - hole_ref[:, pl.ds(at, COLS)]) * factor

    contract(z_ref, table, write)


def local(coef_zero, coef_shift, coupling, partner):
    nrow = lax.axis_size("krow")
    me = lax.axis_index("krow")
    nband = lax.axis_size("band")
    half = lax.axis_index("band")
    nexc = lax.axis_size("exc")
    exc = lax.axis_index("exc")
    mine, nval, ncond, kdev = coef_zero.shape
    nq, share, lower = coef_shift.shape[:3]
    modes = coupling.shape[2]
    cap = kdev // PEERS
    pairs = nval * ncond
    depth = pairs * kdev
    groups = nq // nband
    states = mine * nexc
    kept = states // nrow
    kept_pad = round_up(kept, 8)
    rows = round_up(share, ROWS)
    cols = round_up(modes * rows, COLS)
    scale = (1.0 * pairs * nrow * kdev) ** (-0.5)

    flat = jnp.pad(coef_shift.reshape(nq, share, lower * ncond * kdev), ((0, 0), (0, rows - share), (0, 0)))
    keep = lax.dynamic_slice_in_dim(flat, half * groups, groups, axis=0)
    give = lax.dynamic_slice_in_dim(flat, (nband - 1 - half) * groups, groups, axis=0)
    got = lax.ppermute(give, "band", [(0, 1), (1, 0)])
    first = half == 0
    full = jnp.concatenate([jnp.where(first, keep, got), jnp.where(first, got, keep)], axis=2)

    part = lax.dynamic_slice_in_dim(partner, half * groups, groups, axis=0)
    owner = (part // kdev).reshape(groups, nrow, kdev)
    within = (part % kdev).reshape(groups, nrow, kdev)
    ids = jnp.arange(kdev, dtype=jnp.int32)
    slots = jnp.arange(cap, dtype=jnp.int32)
    tri = (ids[:, None] <= ids[None, :]).astype(jnp.bfloat16)
    eye = jnp.eye(ncond, dtype=jnp.bfloat16)

    def ranked(flags):
        counts = jnp.einsum("qdk,kl->qdl", flags.astype(jnp.bfloat16), tri, preferred_element_type=jnp.float32)
        return flags[..., None] & (counts.astype(jnp.int32)[..., None] - 1 == slots)

    chosen = ranked(owner == me).astype(jnp.bfloat16)
    places = (within[..., None] == ids).astype(jnp.bfloat16)
    select = jnp.einsum("qdkx,qdkj->qdxj", places, chosen, preferred_element_type=jnp.float32).astype(jnp.bfloat16)
    select = (eye[:, None, :, None] * select[:, :, None, :, None, :]).reshape(
        groups, nrow, ncond * kdev, ncond * cap
    )
    my_owner = lax.dynamic_index_in_dim(owner, me, axis=1, keepdims=False)
    match = my_owner[:, None, :] == jnp.arange(nrow, dtype=jnp.int32)[None, :, None]
    perm = jnp.swapaxes(ranked(match), 2, 3).astype(jnp.bfloat16)
    perm = (eye[:, None, :, None] * perm[:, :, None, :, None, :]).reshape(
        groups, nrow * ncond * cap, ncond * kdev
    )

    incoming = []
    for g in range(groups):
        outgoing = pl.pallas_call(
            pick_kernel,
            out_shape=jax.ShapeDtypeStruct((nrow, rows, pairs * cap), jnp.bfloat16),
            compiler_params=pltpu.CompilerParams(vmem_limit_bytes=LIMIT),
            name="pick",
        )(full[g], select[g])
        incoming.append(lax.all_to_all(outgoing, "krow", split_axis=0, concat_axis=0, tiled=True))

    zero = coef_zero.reshape(mine, depth)
    if nexc == 2:
        other = lax.ppermute(zero, "exc", [(0, 1), (1, 0)])
        lead = exc == 0
        whole = jnp.concatenate([jnp.where(lead, zero, other), jnp.where(lead, other, zero)], axis=0)
    else:
        whole = lax.all_gather(zero, "exc", axis=0, tiled=True)
    whole = jnp.pad(whole.reshape(nrow, kept, depth), ((0, 0), (0, kept_pad - kept), (0, 0)))
    whole = whole.reshape(nrow * kept_pad, depth)

    tops = jnp.stack([jnp.max(jnp.abs(a)).astype(jnp.float32) for a in (coef_zero, coef_shift, coupling)])
    tops = lax.pmax(tops, ("krow", "exc", "band"))
    bound = tops[0] * tops[1] * tops[2] * (2.0 * ncond * depth * nrow)
    factor = 32768.0 / jnp.maximum(bound, 1e-30)

    couple = lax.dynamic_slice_in_dim(coupling, half * groups, groups, axis=1).astype(jnp.float32)
    couple = couple.reshape(2, groups, modes * ncond * ncond, 1, kdev)
    couple = jnp.broadcast_to(couple, couple.shape[:3] + (8, kdev))

    macs = rows * modes * depth * 4 + whole.shape[0] * cols * depth
    cost = pl.CostEstimate(flops=8 * macs, bytes_accessed=8 * 2**20, transcendentals=0)
    smem = pl.BlockSpec(memory_space=pltpu.SMEM)
    vmem = pl.BlockSpec(memory_space=pltpu.VMEM)
    partial_shape = jax.ShapeDtypeStruct((nrow * kept_pad, cols), jnp.float32)
    table = pltpu.VMEM((cols, depth), jnp.bfloat16)
    params = pltpu.CompilerParams(vmem_limit_bytes=LIMIT)
    holes = [
        pl.pallas_call(
            functools.partial(hole_kernel, modes, nval, ncond),
            out_shape=partial_shape,
            scratch_shapes=[table],
            compiler_params=params,
            cost_estimate=cost,
            name="hole",
        )(full[g], couple[1, g], whole)
        for g in range(groups)
    ]

    pieces = []
    for g in range(groups):
        partial = pl.pallas_call(
            functools.partial(elec_kernel, modes, nval, ncond),
            out_shape=partial_shape,
            in_specs=[smem] + [vmem] * 5,
            out_specs=vmem,
            scratch_shapes=[pltpu.VMEM((rows, depth), jnp.bfloat16), table],
            compiler_params=params,
            cost_estimate=cost,
            name="elec",
        )(factor.reshape(1), incoming[g], perm[g], couple[0, g], whole, holes[g])
        blocks = partial.reshape(nrow, kept_pad, cols)

        def block(d):
            return lax.dynamic_index_in_dim(blocks, jnp.clip(d, 0, nrow - 1), axis=0, keepdims=False)

        up = down = None
        for t in range(1, nrow):
            send_up, send_down = block(me + nrow - t), block(me - nrow + t)
            if up is not None:
                send_up = send_up + up.astype(jnp.float32)
                send_down = send_down + down.astype(jnp.float32)
            up = lax.ppermute(send_up.astype(jnp.float16), "krow", [(z, z + 1) for z in range(t)])
            down = lax.ppermute(
                send_down.astype(jnp.float16), "krow", [(z, z - 1) for z in range(nrow - t, nrow)]
            )
        total = block(me)
        if up is not None:
            total = total + up.astype(jnp.float32) + down.astype(jnp.float32)
        total = total[:kept, : modes * rows].reshape(kept, modes, rows)[:, :, :share]
        pieces.append(total * (scale / factor))
    return jnp.stack(pieces, axis=1)


def solution(mesh):
    placed = (
        P(("grp", "exc"), None, None, "krow"),
        P(None, ("grp", "exc"), "band", None, "krow"),
        P(None, "grp", None, None, None, "krow"),
        P(),
    )
    return jax.shard_map(
        local,
        mesh=mesh,
        in_specs=placed,
        out_specs=P(("grp", "krow"), "band", None, "exc"),
        check_vma=False,
    )
```

```python
import functools

import jax
import jax.numpy as jnp
from jax import lax
from jax.experimental import pallas as pl
from jax.experimental.pallas import tpu as pltpu
from jax.sharding import PartitionSpec as P

PEERS = 4
ROWS = 16
LANES = 128
COLS = 384
LIMIT = 40 * 2**20


def round_up(n, unit):
    return (n + unit - 1) // unit * unit


def pick_kernel(x_ref, sel_ref, out_ref):
    nrow, width, _ = sel_ref.shape
    wide = sel_ref.shape[2]
    for d in range(nrow):
        for v in range(x_ref.shape[1] // width):
            got = jnp.dot(
                x_ref[:, v * width : (v + 1) * width], sel_ref[d], preferred_element_type=jnp.float32
            )
            out_ref[d, :, v * wide : (v + 1) * wide] = got.astype(jnp.bfloat16)


def build_table(x_ref, c_ref, y_ref, d_ref, table, modes, nval, ncond, lower):
    rows = y_ref.shape[0]

    def chunk(r, carry):
        at = pl.multiple_of(r * ROWS, ROWS)

        def slab(ref, g):
            piece = ref[pl.ds(at, ROWS), g * LANES : (g + 1) * LANES]
            return piece.astype(jnp.float32).reshape(ROWS // 8, 8, LANES)

        for v in range(nval):
            own = [w for w in range(nval) if (w // lower == v // lower) == (x_ref is not None)]
            if x_ref is not None:
                shifted = [slab(x_ref, v * ncond + a) for a in range(ncond)]
            for c in range(ncond):
                held = [slab(y_ref, w * ncond + c) for w in own]
                for m in range(modes):
                    total = None
                    for w, one in zip(own, held):
                        term = one * d_ref[(m * nval + v) * nval + w][None]
                        total = term if total is None else total + term
                    if x_ref is not None:
                        elec = None
                        for a in range(ncond):
                            term = shifted[a] * c_ref[(m * ncond + a) * ncond + c][None]
                            elec = term if elec is None else elec + term
                        total = elec - total
                    g = v * ncond + c
                    table[pl.ds(m * rows + at, ROWS), g * LANES : (g + 1) * LANES] = total.reshape(
                        ROWS, LANES
                    ).astype(jnp.bfloat16)
        return carry

    lax.fori_loop(0, rows // ROWS, chunk, 0)
    used = modes * rows
    if used < table.shape[0]:
        table[used:, :] = jnp.zeros((table.shape[0] - used, table.shape[1]), jnp.bfloat16)


def contract(z_ref, table, write):
    def cols(j, carry):
        at = pl.multiple_of(j * COLS, COLS)
        write(
            at,
            lax.dot_general(
                z_ref[...],
                table[pl.ds(at, COLS), :],
                (((1,), (1,)), ((), ())),
                preferred_element_type=jnp.float32,
            ),
        )
        return carry

    lax.fori_loop(0, table.shape[0] // COLS, cols, 0)


def hole_kernel(modes, nval, ncond, lower, y_ref, d_ref, z_ref, out_ref, table):
    build_table(None, None, y_ref, d_ref, table, modes, nval, ncond, lower)

    def write(at, got):
        out_ref[:, pl.ds(at, COLS)] = got

    contract(z_ref, table, write)


def elec_kernel(
    modes, nval, ncond, lower, inc_ref, perm_ref, c_ref, y_ref, d_ref, z_ref, hole_ref, out_ref, x_ref, table
):
    nrow = inc_ref.shape[0]
    wide = inc_ref.shape[2] // nval
    width = perm_ref.shape[1]
    for v in range(nval):
        got = jnp.zeros((x_ref.shape[0], width), jnp.float32)
        for o in range(nrow):
            got = got + jnp.dot(
                inc_ref[o, :, v * wide : (v + 1) * wide],
                perm_ref[o * wide : (o + 1) * wide, :],
                preferred_element_type=jnp.float32,
            )
        x_ref[:, v * width : (v + 1) * width] = got.astype(jnp.bfloat16)
    build_table(x_ref, c_ref, y_ref, d_ref, table, modes, nval, ncond, lower)

    def write(at, got):
        out_ref[:, pl.ds(at, COLS)] = got - hole_ref[:, pl.ds(at, COLS)]

    contract(z_ref, table, write)


def local(coef_zero, coef_shift, coupling, partner):
    nrow = lax.axis_size("krow")
    me = lax.axis_index("krow")
    nband = lax.axis_size("band")
    half = lax.axis_index("band")
    nexc = lax.axis_size("exc")
    exc = lax.axis_index("exc")
    mine, nval, ncond, kdev = coef_zero.shape
    nq, share, lower = coef_shift.shape[:3]
    modes = coupling.shape[2]
    cap = kdev // PEERS
    pairs = nval * ncond
    depth = pairs * kdev
    groups = nq // nband
    states = mine * nexc
    kept = states // nrow
    kept_pad = round_up(kept, 8)
    rows = round_up(share, ROWS)
    cols = round_up(modes * rows, COLS)
    scale = (1.0 * pairs * nrow * kdev) ** (-0.5)

    flat = jnp.pad(coef_shift.reshape(nq, share, lower * ncond * kdev), ((0, 0), (0, rows - share), (0, 0)))
    keep = lax.dynamic_slice_in_dim(flat, half * groups, groups, axis=0)
    give = lax.dynamic_slice_in_dim(flat, (nband - 1 - half) * groups, groups, axis=0)
    got = lax.ppermute(give, "band", [(0, 1), (1, 0)])
    first = half == 0
    full = jnp.concatenate([jnp.where(first, keep, got), jnp.where(first, got, keep)], axis=2)

    part = lax.dynamic_slice_in_dim(partner, half * groups, groups, axis=0)
    owner = (part // kdev).reshape(groups, nrow, kdev)
    within = (part % kdev).reshape(groups, nrow, kdev)
    ids = jnp.arange(kdev, dtype=jnp.int32)
    slots = jnp.arange(cap, dtype=jnp.int32)
    tri = (ids[:, None] <= ids[None, :]).astype(jnp.bfloat16)
    eye = jnp.eye(ncond, dtype=jnp.bfloat16)

    def ranked(flags):
        counts = jnp.einsum("qdk,kl->qdl", flags.astype(jnp.bfloat16), tri, preferred_element_type=jnp.float32)
        return flags[..., None] & (counts.astype(jnp.int32)[..., None] - 1 == slots)

    chosen = ranked(owner == me).astype(jnp.bfloat16)
    places = (within[..., None] == ids).astype(jnp.bfloat16)
    select = jnp.einsum("qdkx,qdkj->qdxj", places, chosen, preferred_element_type=jnp.float32).astype(jnp.bfloat16)
    select = (eye[:, None, :, None] * select[:, :, None, :, None, :]).reshape(
        groups, nrow, ncond * kdev, ncond * cap
    )
    my_owner = lax.dynamic_index_in_dim(owner, me, axis=1, keepdims=False)
    match = my_owner[:, None, :] == jnp.arange(nrow, dtype=jnp.int32)[None, :, None]
    perm = jnp.swapaxes(ranked(match), 2, 3).astype(jnp.bfloat16)
    perm = (eye[:, None, :, None] * perm[:, :, None, :, None, :]).reshape(
        groups, nrow * ncond * cap, ncond * kdev
    )

    incoming = []
    for g in range(groups):
        outgoing = pl.pallas_call(
            pick_kernel,
            out_shape=jax.ShapeDtypeStruct((nrow, rows, pairs * cap), jnp.bfloat16),
            compiler_params=pltpu.CompilerParams(vmem_limit_bytes=LIMIT),
            name="pick",
        )(full[g], select[g])
        incoming.append(lax.all_to_all(outgoing, "krow", split_axis=0, concat_axis=0, tiled=True))

    zero = coef_zero.reshape(mine, depth)
    if nexc == 2:
        other = lax.ppermute(zero, "exc", [(0, 1), (1, 0)])
        lead = exc == 0
        whole = jnp.concatenate([jnp.where(lead, zero, other), jnp.where(lead, other, zero)], axis=0)
    else:
        whole = lax.all_gather(zero, "exc", axis=0, tiled=True)
    whole = jnp.pad(whole.reshape(nrow, kept, depth), ((0, 0), (0, kept_pad - kept), (0, 0)))
    whole = whole.reshape(nrow * kept_pad, depth)

    couple = lax.dynamic_slice_in_dim(coupling, half * groups, groups, axis=1).astype(jnp.float32)
    couple = couple.reshape(2, groups, modes * ncond * ncond, 1, kdev)
    couple = jnp.broadcast_to(couple, couple.shape[:3] + (8, kdev))

    macs = rows * modes * depth * 4 + whole.shape[0] * cols * depth
    cost = pl.CostEstimate(flops=8 * macs, bytes_accessed=8 * 2**20, transcendentals=0)
    partial_shape = jax.ShapeDtypeStruct((nrow * kept_pad, cols), jnp.float32)
    table = pltpu.VMEM((cols, depth), jnp.bfloat16)
    params = pltpu.CompilerParams(vmem_limit_bytes=LIMIT)
    holes = [
        pl.pallas_call(
            functools.partial(hole_kernel, modes, nval, ncond, lower),
            out_shape=partial_shape,
            scratch_shapes=[table],
            compiler_params=params,
            cost_estimate=cost,
            name="hole",
        )(full[g], couple[1, g], whole)
        for g in range(groups)
    ]

    pieces = []
    for g in range(groups):
        partial = pl.pallas_call(
            functools.partial(elec_kernel, modes, nval, ncond, lower),
            out_shape=partial_shape,
            scratch_shapes=[pltpu.VMEM((rows, depth), jnp.bfloat16), table],
            compiler_params=params,
            cost_estimate=cost,
            name="elec",
        )(incoming[g], perm[g], couple[0, g], full[g], couple[1, g], whole, holes[g])
        blocks = partial.reshape(nrow, kept_pad, cols)

        def block(d):
            return lax.dynamic_index_in_dim(blocks, jnp.clip(d, 0, nrow - 1), axis=0, keepdims=False)

        up = down = None
        for t in range(1, nrow):
            send_up, send_down = block(me + nrow - t), block(me - nrow + t)
            if up is not None:
                send_up = send_up + up.astype(jnp.float32)
                send_down = send_down + down.astype(jnp.float32)
            up = lax.ppermute(send_up.astype(jnp.bfloat16), "krow", [(z, z + 1) for z in range(t)])
            down = lax.ppermute(
                send_down.astype(jnp.bfloat16), "krow", [(z, z - 1) for z in range(nrow - t, nrow)]
            )
        total = block(me)
        if up is not None:
            total = total + up.astype(jnp.float32) + down.astype(jnp.float32)
        total = total[:kept, : modes * rows].reshape(kept, modes, rows)[:, :, :share]
        pieces.append(total * scale)
    return jnp.stack(pieces, axis=1)


def solution(mesh):
    placed = (
        P(("grp", "exc"), None, None, "krow"),
        P(None, ("grp", "exc"), "band", None, "krow"),
        P(None, "grp", None, None, None, "krow"),
        P(),
    )
    return jax.shard_map(
        local,
        mesh=mesh,
        in_specs=placed,
        out_specs=P(("grp", "krow"), "band", None, "exc"),
        check_vma=False,
    )
```

```python
import functools

import jax
import jax.numpy as jnp
from jax import lax
from jax.experimental import pallas as pl
from jax.experimental.pallas import tpu as pltpu
from jax.sharding import PartitionSpec as P

PEERS = 4
ROWS = 16
LANES = 128
COLS = 384
LIMIT = 56 * 2**20
MESH = pl.DeviceIdType.MESH


def round_up(n, unit):
    return (n + unit - 1) // unit * unit


def build_table(x_ref, c_ref, y_ref, d_ref, table, modes, nval, ncond, lower):
    rows = y_ref.shape[1]

    def chunk(r, carry):
        at = pl.multiple_of(r * ROWS, ROWS)

        def slab(ref, g):
            piece = ref[pl.ds(at, ROWS), g * LANES : (g + 1) * LANES]
            return piece.astype(jnp.float32).reshape(ROWS // 8, 8, LANES)

        for v in range(nval):
            own = [w for w in range(nval) if (w // lower == v // lower) == (x_ref is not None)]
            if x_ref is not None:
                shifted = [slab(x_ref, v * ncond + a) for a in range(ncond)]
            for c in range(ncond):
                held = [slab(y_ref.at[w // lower], w % lower * ncond + c) for w in own]
                for m in range(modes):
                    total = None
                    for w, one in zip(own, held):
                        term = one * d_ref[(m * nval + v) * nval + w][None]
                        total = term if total is None else total + term
                    if x_ref is not None:
                        elec = None
                        for a in range(ncond):
                            term = shifted[a] * c_ref[(m * ncond + a) * ncond + c][None]
                            elec = term if elec is None else elec + term
                        total = elec - total
                    g = v * ncond + c
                    table[pl.ds(m * rows + at, ROWS), g * LANES : (g + 1) * LANES] = total.reshape(
                        ROWS, LANES
                    ).astype(jnp.bfloat16)
        return carry

    lax.fori_loop(0, rows // ROWS, chunk, 0)
    used = modes * rows
    if used < table.shape[0]:
        table[used:, :] = jnp.zeros((table.shape[0] - used, table.shape[1]), jnp.bfloat16)


def contract(z_ref, table, write):
    def cols(j, carry):
        at = pl.multiple_of(j * COLS, COLS)
        write(
            at,
            lax.dot_general(
                z_ref[...],
                table[pl.ds(at, COLS), :],
                (((1,), (1,)), ((), ())),
                preferred_element_type=jnp.float32,
            ),
        )
        return carry

    lax.fori_loop(0, table.shape[0] // COLS, cols, 0)


def main_kernel(
    dims, zero_ref, flat_ref, sel_ref, perm_ref, c_ref, d_ref, out_ref,
    zbuf, full, outgo, inc, x_ref, table, part, up_out, up_in, down_out, down_in,
    local_sem, band_sem, exc_send, exc_recv, go_send, go_recv, up_send, up_recv, down_send, down_recv,
):
    modes, nval, ncond, lower, groups, kept_pad, nrow, nexc, scale = dims
    me, exc, half = lax.axis_index("krow"), lax.axis_index("exc"), lax.axis_index("band")
    width, wide = sel_ref.shape[2:]
    zrows = zero_ref.shape[0]
    last = nrow - 1

    barrier = pltpu.get_barrier_semaphore()
    for s in range(1, nrow):
        pl.semaphore_signal(barrier, inc=1, device_id={"krow": lax.rem(me + s, nrow)}, device_id_type=MESH)
    for s in range(1, nexc):
        pl.semaphore_signal(barrier, inc=1, device_id={"exc": lax.rem(exc + s, nexc)}, device_id_type=MESH)
    pl.semaphore_signal(barrier, inc=1, device_id={"band": 1 - half}, device_id_type=MESH)
    pl.semaphore_wait(barrier, nrow - 1 + nexc - 1 + 1)

    own_full = pltpu.make_async_copy(flat_ref.at[pl.ds(half * groups, groups)], full.at[half], local_sem.at[0])
    band_copy = pltpu.make_async_remote_copy(
        src_ref=flat_ref.at[pl.ds((1 - half) * groups, groups)],
        dst_ref=full.at[half],
        send_sem=band_sem.at[0],
        recv_sem=band_sem.at[1],
        device_id={"band": 1 - half},
        device_id_type=MESH,
    )
    band_copy.start()
    own_full.start()
    place = pl.ds(pl.multiple_of(exc * zrows, 16), zrows)
    own_zero = pltpu.make_async_copy(zero_ref, zbuf.at[place], local_sem.at[1])
    own_zero.start()
    zero_copies = [
        pltpu.make_async_remote_copy(
            src_ref=zero_ref,
            dst_ref=zbuf.at[place],
            send_sem=exc_send.at[s],
            recv_sem=exc_recv.at[s],
            device_id={"exc": lax.rem(exc + s, nexc)},
            device_id_type=MESH,
        )
        for s in range(1, nexc)
    ]
    for copy in zero_copies:
        copy.start()
    own_full.wait()
    band_copy.wait()

    go_copies = []
    for g in range(groups):
        row = [None]
        for s in list(range(1, nrow)) + [0]:
            dest = lax.rem(me + s, nrow)
            target = outgo if s else inc
            for v in range(nval):
                at = v % lower * width
                got = jnp.dot(
                    full[v // lower, g, :, at : at + width], sel_ref[g, dest], preferred_element_type=jnp.float32
                )
                target[g, s, :, v * wide : (v + 1) * wide] = got.astype(jnp.bfloat16)
            if s:
                copy = pltpu.make_async_remote_copy(
                    src_ref=outgo.at[g, s],
                    dst_ref=inc.at[g, s],
                    send_sem=go_send.at[g, s],
                    recv_sem=go_recv.at[g, s],
                    device_id={"krow": dest},
                    device_id_type=MESH,
                )
                copy.start()
                row.append(copy)
        go_copies.append(row)

    def contract(write):
        def cols(j, carry):
            at = pl.multiple_of(j * COLS, COLS)
            got = lax.dot_general(
                zbuf[...], table[pl.ds(at, COLS), :], (((1,), (1,)), ((), ())), preferred_element_type=jnp.float32
            )
            write(at, got)
            return carry

        lax.fori_loop(0, table.shape[0] // COLS, cols, 0)

    for g in range(groups):
        build_table(None, None, full.at[:, g], d_ref.at[g], table, modes, nval, ncond, lower)
        if g == 0:
            own_zero.wait()
            for copy in zero_copies:
                copy.wait()

        def first_part(at, got, g=g):
            part[g, :, pl.ds(at, COLS)] = -got

        contract(first_part)

    def neighbour(g, t, out, into, send, recv, device):
        return pltpu.make_async_remote_copy(
            src_ref=out.at[g, t],
            dst_ref=into.at[g, t],
            send_sem=send.at[g, t],
            recv_sem=recv.at[g, t],
            device_id={"krow": device},
            device_id_type=MESH,
        )

    def flow(up):
        if up:
            return me, lambda t: me + nrow - t, lambda g, t: neighbour(
                g, t - 1, up_out, up_in, up_send, up_recv, lax.rem(me + 1, nrow)
            )
        return last - me, lambda t: me - nrow + t, lambda g, t: neighbour(
            g, t - 1, down_out, down_in, down_send, down_recv, lax.rem(me + last, nrow)
        )

    def step(g, t):
        for up in (True, False):
            pos, block, copy = flow(up)
            out, into = (up_out, up_in) if up else (down_out, down_in)

            def mine(block=block):
                d = jnp.clip(block(t), 0, last)
                return part[g, pl.ds(pl.multiple_of(d * kept_pad, 16), kept_pad), :]

            @pl.when(pos == 0)
            def _(out=out, copy=copy, mine=mine):
                out[g, t - 1] = mine().astype(jnp.bfloat16)
                copy(g, t).start()

            if t > 1:

                @pl.when((pos >= 1) & (pos <= t - 1))
                def _(out=out, into=into, copy=copy, mine=mine):
                    copy(g, t - 1).wait_recv()
                    out[g, t - 1] = (mine() + into[g, t - 2].astype(jnp.float32)).astype(jnp.bfloat16)
                    copy(g, t).start()

    def finish(g):
        out_ref[g] = part[g, pl.ds(pl.multiple_of(me * kept_pad, 16), kept_pad), :] * scale
        for up in (True, False):
            pos, _, copy = flow(up)
            into = up_in if up else down_in

            @pl.when(pos >= 1)
            def _(into=into, copy=copy):
                copy(g, last).wait_recv()
                out_ref[g] = out_ref[g] + into[g, last - 1].astype(jnp.float32) * scale

    def elec(g, between):
        for copy in go_copies[g][1:]:
            copy.wait_recv()
        for v in range(nval):
            got = jnp.zeros((x_ref.shape[0], width), jnp.float32)
            for s in range(nrow):
                owner = lax.rem(me + nrow - s, nrow)
                got = got + jnp.dot(
                    inc[g, s, :, v * wide : (v + 1) * wide], perm_ref[g, owner], preferred_element_type=jnp.float32
                )
            x_ref[:, v * width : (v + 1) * width] = got.astype(jnp.bfloat16)
        build_table(x_ref, c_ref.at[g], full.at[:, g], d_ref.at[g], table, modes, nval, ncond, lower)
        between()

        def add_part(at, got):
            part[g, :, pl.ds(at, COLS)] = part[g, :, pl.ds(at, COLS)] + got

        contract(add_part)

    for g in range(groups):

        def between(g=g):
            if g > 0 and nrow > 2:
                step(g - 1, 2)

        elec(g, between)
        step(g, 1)
        if g > 0:
            for t in range(3, nrow):
                step(g - 1, t)
            finish(g - 1)
    for t in range(2, nrow):
        step(groups - 1, t)
    finish(groups - 1)

    for g in range(groups):
        for copy in go_copies[g][1:]:
            copy.wait_send()
        for t in range(1, nrow):
            for up in (True, False):
                pos, _, copy = flow(up)

                @pl.when(pos <= t - 1)
                def _(copy=copy):
                    copy(g, t).wait_send()


def local(coef_zero, coef_shift, coupling, partner):
    nrow = lax.axis_size("krow")
    me = lax.axis_index("krow")
    nband = lax.axis_size("band")
    half = lax.axis_index("band")
    nexc = lax.axis_size("exc")
    mine, nval, ncond, kdev = coef_zero.shape
    nq, share, lower = coef_shift.shape[:3]
    modes = coupling.shape[2]
    cap = kdev // PEERS
    pairs = nval * ncond
    depth = pairs * kdev
    groups = nq // nband
    kept = mine * nexc // nrow
    held = mine // kept
    kept_pad = round_up(kept, ROWS)
    rows = round_up(share, ROWS)
    cols = round_up(modes * rows, COLS)
    scale = (1.0 * pairs * nrow * kdev) ** (-0.5)

    flat = jnp.pad(coef_shift.reshape(nq, share, lower * ncond * kdev), ((0, 0), (0, rows - share), (0, 0)))
    zero = jnp.pad(coef_zero.reshape(held, kept, depth), ((0, 0), (0, kept_pad - kept), (0, 0)))
    zero = zero.reshape(held * kept_pad, depth)

    part = lax.dynamic_slice_in_dim(partner, half * groups, groups, axis=0)
    owner = (part // kdev).reshape(groups, nrow, kdev)
    within = (part % kdev).reshape(groups, nrow, kdev)
    ids = jnp.arange(kdev, dtype=jnp.int32)
    slots = jnp.arange(cap, dtype=jnp.int32)
    tri = (ids[:, None] <= ids[None, :]).astype(jnp.bfloat16)
    eye = jnp.eye(ncond, dtype=jnp.bfloat16)

    def ranked(flags):
        counts = jnp.einsum("qdk,kl->qdl", flags.astype(jnp.bfloat16), tri, preferred_element_type=jnp.float32)
        return flags[..., None] & (counts.astype(jnp.int32)[..., None] - 1 == slots)

    chosen = ranked(owner == me).astype(jnp.bfloat16)
    places = (within[..., None] == ids).astype(jnp.bfloat16)
    select = jnp.einsum("qdkx,qdkj->qdxj", places, chosen, preferred_element_type=jnp.float32).astype(jnp.bfloat16)
    select = (eye[:, None, :, None] * select[:, :, None, :, None, :]).reshape(
        groups, nrow, ncond * kdev, ncond * cap
    )
    my_owner = lax.dynamic_index_in_dim(owner, me, axis=1, keepdims=False)
    match = my_owner[:, None, :] == jnp.arange(nrow, dtype=jnp.int32)[None, :, None]
    perm = jnp.swapaxes(ranked(match), 2, 3).astype(jnp.bfloat16)
    perm = (eye[:, None, :, None] * perm[:, :, None, :, None, :]).reshape(
        groups, nrow, ncond * cap, ncond * kdev
    )

    couple = lax.dynamic_slice_in_dim(coupling, half * groups, groups, axis=1).astype(jnp.float32)
    couple = couple.reshape(2, groups, modes * ncond * ncond, 1, kdev)
    couple = jnp.broadcast_to(couple, couple.shape[:3] + (8, kdev))

    macs = groups * (rows * modes * depth * 4 + 2 * nrow * kept_pad * cols * depth)
    hbm, vmem = pl.BlockSpec(memory_space=pl.ANY), pl.BlockSpec(memory_space=pltpu.VMEM)
    hops = pltpu.VMEM((groups, nrow - 1, kept_pad, cols), jnp.bfloat16)
    parcels = pltpu.VMEM((groups, nrow, rows, pairs * cap), jnp.bfloat16)
    done = pl.pallas_call(
        functools.partial(main_kernel, (modes, nval, ncond, lower, groups, kept_pad, nrow, nexc, scale)),
        out_shape=jax.ShapeDtypeStruct((groups, kept_pad, cols), jnp.float32),
        in_specs=[hbm, hbm, vmem, vmem, vmem, vmem],
        out_specs=vmem,
        scratch_shapes=[
            pltpu.VMEM((nrow * kept_pad, depth), jnp.bfloat16),
            pltpu.VMEM((nband, groups, rows, lower * ncond * kdev), jnp.bfloat16),
            parcels,
            parcels,
            pltpu.VMEM((rows, depth), jnp.bfloat16),
            pltpu.VMEM((cols, depth), jnp.bfloat16),
            pltpu.VMEM((groups, nrow * kept_pad, cols), jnp.float32),
            hops,
            hops,
            hops,
            hops,
            pltpu.SemaphoreType.DMA((2,)),
            pltpu.SemaphoreType.DMA((2,)),
            pltpu.SemaphoreType.DMA((nexc,)),
            pltpu.SemaphoreType.DMA((nexc,)),
        ]
        + [pltpu.SemaphoreType.DMA((groups, nrow))] * 6,
        compiler_params=pltpu.CompilerParams(vmem_limit_bytes=LIMIT, collective_id=0, has_side_effects=True),
        cost_estimate=pl.CostEstimate(flops=2 * macs, bytes_accessed=16 * 2**20, transcendentals=0),
        name="coupling",
    )(zero, flat, select, perm, couple[0], couple[1])
    done = done[:, :kept, : modes * rows].reshape(groups, kept, modes, rows)[..., :share]
    return jnp.swapaxes(done, 0, 1)


def solution(mesh):
    placed = (
        P(("grp", "exc"), None, None, "krow"),
        P(None, ("grp", "exc"), "band", None, "krow"),
        P(None, "grp", None, None, None, "krow"),
        P(),
    )
    return jax.shard_map(
        local,
        mesh=mesh,
        in_specs=placed,
        out_specs=P(("grp", "krow"), "band", None, "exc"),
        check_vma=False,
    )
```

```python
import functools

import jax
import jax.numpy as jnp
from jax import lax
from jax.experimental import pallas as pl
from jax.experimental.pallas import tpu as pltpu
from jax.sharding import PartitionSpec as P

PEERS = 4
ROWS = 16
LANES = 128
COLS = 384
LIMIT = 56 * 2**20
MESH = pl.DeviceIdType.MESH


def round_up(n, unit):
    return (n + unit - 1) // unit * unit


def build_table(x_ref, c_ref, y_ref, d_ref, table, modes, nval, ncond, lower):
    rows = y_ref.shape[1]

    def chunk(r, carry):
        at = pl.multiple_of(r * ROWS, ROWS)

        def slab(ref, g):
            piece = ref[pl.ds(at, ROWS), g * LANES : (g + 1) * LANES]
            return piece.astype(jnp.float32).reshape(ROWS // 8, 8, LANES)

        for v in range(nval):
            own = [w for w in range(nval) if (w // lower == v // lower) == (x_ref is not None)]
            if x_ref is not None:
                shifted = [slab(x_ref, v * ncond + a) for a in range(ncond)]
            for c in range(ncond):
                held = [slab(y_ref.at[w // lower], w % lower * ncond + c) for w in own]
                for m in range(modes):
                    total = None
                    for w, one in zip(own, held):
                        term = one * d_ref[(m * nval + v) * nval + w][None]
                        total = term if total is None else total + term
                    if x_ref is not None:
                        elec = None
                        for a in range(ncond):
                            term = shifted[a] * c_ref[(m * ncond + a) * ncond + c][None]
                            elec = term if elec is None else elec + term
                        total = elec - total
                    g = v * ncond + c
                    table[pl.ds(m * rows + at, ROWS), g * LANES : (g + 1) * LANES] = total.reshape(
                        ROWS, LANES
                    ).astype(jnp.bfloat16)
        return carry

    lax.fori_loop(0, rows // ROWS, chunk, 0)
    used = modes * rows
    if used < table.shape[0]:
        table[used:, :] = jnp.zeros((table.shape[0] - used, table.shape[1]), jnp.bfloat16)


def contract(z_ref, table, write):
    def cols(j, carry):
        at = pl.multiple_of(j * COLS, COLS)
        write(
            at,
            lax.dot_general(
                z_ref[...],
                table[pl.ds(at, COLS), :],
                (((1,), (1,)), ((), ())),
                preferred_element_type=jnp.float32,
            ),
        )
        return carry

    lax.fori_loop(0, table.shape[0] // COLS, cols, 0)


def main_kernel(
    dims, zero_ref, flat_ref, sel_small, perm_small, c_small, d_small, out_ref,
    sel_ref, perm_ref, c_ref, d_ref, zbuf, full, outgo, inc, x_ref, table, part, up_out, up_in, down_out, down_in,
    local_sem, band_sem, exc_send, exc_recv, go_send, go_recv, up_send, up_recv, down_send, down_recv,
):
    modes, nval, ncond, lower, groups, kept_pad, share, nrow, nexc, scale = dims
    me, exc, half = lax.axis_index("krow"), lax.axis_index("exc"), lax.axis_index("band")
    width, wide = sel_ref.shape[2:]
    zrows = zero_ref.shape[0]
    last = nrow - 1

    barrier = pltpu.get_barrier_semaphore()
    for s in range(1, nrow):
        pl.semaphore_signal(barrier, inc=1, device_id={"krow": lax.rem(me + s, nrow)}, device_id_type=MESH)
    for s in range(1, nexc):
        pl.semaphore_signal(barrier, inc=1, device_id={"exc": lax.rem(exc + s, nexc)}, device_id_type=MESH)
    pl.semaphore_signal(barrier, inc=1, device_id={"band": 1 - half}, device_id_type=MESH)
    pl.semaphore_wait(barrier, nrow - 1 + nexc - 1 + 1)

    own_full = pltpu.make_async_copy(flat_ref.at[pl.ds(half * groups, groups)], full.at[half], local_sem.at[0])
    band_copy = pltpu.make_async_remote_copy(
        src_ref=flat_ref.at[pl.ds((1 - half) * groups, groups)],
        dst_ref=full.at[half],
        send_sem=band_sem.at[0],
        recv_sem=band_sem.at[1],
        device_id={"band": 1 - half},
        device_id_type=MESH,
    )
    band_copy.start()
    own_full.start()
    place = pl.ds(pl.multiple_of(exc * zrows, 16), zrows)
    own_zero = pltpu.make_async_copy(zero_ref, zbuf.at[place], local_sem.at[1])
    own_zero.start()
    zero_copies = [
        pltpu.make_async_remote_copy(
            src_ref=zero_ref,
            dst_ref=zbuf.at[place],
            send_sem=exc_send.at[s],
            recv_sem=exc_recv.at[s],
            device_id={"exc": lax.rem(exc + s, nexc)},
            device_id_type=MESH,
        )
        for s in range(1, nexc)
    ]
    for copy in zero_copies:
        copy.start()
    sel_ref[...] = jnp.zeros(sel_ref.shape, sel_ref.dtype)
    perm_ref[...] = jnp.zeros(perm_ref.shape, perm_ref.dtype)
    tall, thin = sel_small.shape[2:]
    for g in range(groups):
        for d in range(nrow):
            for c in range(ncond):
                long, short = slice(c * tall, (c + 1) * tall), slice(c * thin, (c + 1) * thin)
                sel_ref[g, d, long, short] = sel_small[g, d]
                perm_ref[g, d, short, long] = perm_small[g, d]

        def spread(i, carry, g=g):
            c_ref[g, i] = jnp.broadcast_to(c_small[g, pl.ds(i, 1), :], c_ref.shape[2:])
            d_ref[g, i] = jnp.broadcast_to(d_small[g, pl.ds(i, 1), :], d_ref.shape[2:])
            return carry

        lax.fori_loop(0, c_small.shape[1], spread, 0)
    chunks = table.shape[0] // COLS
    used = chunks * kept_pad
    if used < part.shape[2]:
        part[:, :, used:, :] = jnp.zeros(part.shape[:2] + (part.shape[2] - used, COLS), jnp.float32)
    own_full.wait()
    band_copy.wait()

    go_copies = []
    for g in range(groups):
        row = [None]
        for s in list(range(1, nrow)) + [0]:
            dest = lax.rem(me + s, nrow)
            target = outgo if s else inc
            for v in range(nval):
                at = v % lower * width
                got = jnp.dot(
                    full[v // lower, g, :, at : at + width], sel_ref[g, dest], preferred_element_type=jnp.float32
                )
                target[g, s, :, v * wide : (v + 1) * wide] = got.astype(jnp.bfloat16)
            if s:
                copy = pltpu.make_async_remote_copy(
                    src_ref=outgo.at[g, s],
                    dst_ref=inc.at[g, s],
                    send_sem=go_send.at[g, s],
                    recv_sem=go_recv.at[g, s],
                    device_id={"krow": dest},
                    device_id_type=MESH,
                )
                copy.start()
                row.append(copy)
        go_copies.append(row)

    def contract(write):
        def cols(j, carry):
            at = pl.multiple_of(j * COLS, COLS)
            got = lax.dot_general(
                zbuf[...], table[pl.ds(at, COLS), :], (((1,), (1,)), ((), ())), preferred_element_type=jnp.float32
            )
            for d in range(nrow):
                write(d, pl.ds(pl.multiple_of(j * kept_pad, 8), kept_pad), got[d * kept_pad : (d + 1) * kept_pad])
            return carry

        lax.fori_loop(0, chunks, cols, 0)

    for g in range(groups):
        build_table(None, None, full.at[:, g], d_ref.at[g], table, modes, nval, ncond, lower)
        if g == 0:
            own_zero.wait()
            for copy in zero_copies:
                copy.wait()

        def first_part(d, at, got, g=g):
            part[g, d, at, :] = -got

        contract(first_part)

    def neighbour(g, t, out, into, send, recv, device):
        return pltpu.make_async_remote_copy(
            src_ref=out.at[g, t],
            dst_ref=into.at[g, t],
            send_sem=send.at[g, t],
            recv_sem=recv.at[g, t],
            device_id={"krow": device},
            device_id_type=MESH,
        )

    def flow(up):
        if up:
            return me, lambda t: me + nrow - t, lambda g, t: neighbour(
                g, t - 1, up_out, up_in, up_send, up_recv, lax.rem(me + 1, nrow)
            )
        return last - me, lambda t: me - nrow + t, lambda g, t: neighbour(
            g, t - 1, down_out, down_in, down_send, down_recv, lax.rem(me + last, nrow)
        )

    def step(g, t):
        for up in (True, False):
            pos, block, copy = flow(up)
            out, into = (up_out, up_in) if up else (down_out, down_in)

            def mine(block=block):
                return part[g, jnp.clip(block(t), 0, last)]

            @pl.when(pos == 0)
            def _(out=out, copy=copy, mine=mine):
                out[g, t - 1] = mine().astype(jnp.bfloat16)
                copy(g, t).start()

            if t > 1:

                @pl.when((pos >= 1) & (pos <= t - 1))
                def _(out=out, into=into, copy=copy, mine=mine):
                    copy(g, t - 1).wait_recv()
                    out[g, t - 1] = (mine() + into[g, t - 2].astype(jnp.float32)).astype(jnp.bfloat16)
                    copy(g, t).start()

    def finish(g):
        for up in (True, False):
            pos, _, copy = flow(up)
            into = up_in if up else down_in

            @pl.when(pos >= 1)
            def _(into=into, copy=copy):
                copy(g, last).wait_recv()
                part[g, me] = part[g, me] + into[g, last - 1].astype(jnp.float32)

        total = jnp.concatenate(
            [part[g, me, j * kept_pad : (j + 1) * kept_pad, :] for j in range(chunks)], axis=1
        )
        rows = x_ref.shape[0]
        for m in range(modes):
            out_ref[g, m] = total[:, m * rows : m * rows + share] * scale

    def elec(g, between):
        for copy in go_copies[g][1:]:
            copy.wait_recv()
        for v in range(nval):
            got = jnp.zeros((x_ref.shape[0], width), jnp.float32)
            for s in range(nrow):
                owner = lax.rem(me + nrow - s, nrow)
                got = got + jnp.dot(
                    inc[g, s, :, v * wide : (v + 1) * wide], perm_ref[g, owner], preferred_element_type=jnp.float32
                )
            x_ref[:, v * width : (v + 1) * width] = got.astype(jnp.bfloat16)
        build_table(x_ref, c_ref.at[g], full.at[:, g], d_ref.at[g], table, modes, nval, ncond, lower)
        between()

        def add_part(d, at, got):
            part[g, d, at, :] = part[g, d, at, :] + got

        contract(add_part)

    for g in range(groups):

        def between(g=g):
            if g > 0 and nrow > 2:
                step(g - 1, 2)

        elec(g, between)
        step(g, 1)
        if g > 0:
            for t in range(3, nrow):
                step(g - 1, t)
            finish(g - 1)
    for t in range(2, nrow):
        step(groups - 1, t)
    finish(groups - 1)

    for g in range(groups):
        for copy in go_copies[g][1:]:
            copy.wait_send()
        for t in range(1, nrow):
            for up in (True, False):
                pos, _, copy = flow(up)

                @pl.when(pos <= t - 1)
                def _(copy=copy):
                    copy(g, t).wait_send()


def local(coef_zero, coef_shift, coupling, partner):
    nrow = lax.axis_size("krow")
    me = lax.axis_index("krow")
    nband = lax.axis_size("band")
    half = lax.axis_index("band")
    nexc = lax.axis_size("exc")
    mine, nval, ncond, kdev = coef_zero.shape
    nq, share, lower = coef_shift.shape[:3]
    modes = coupling.shape[2]
    cap = kdev // PEERS
    pairs = nval * ncond
    depth = pairs * kdev
    groups = nq // nband
    kept = mine * nexc // nrow
    held = mine // kept
    kept_pad = round_up(kept, 8)
    wire = round_up(kept_pad * (round_up(modes * round_up(share, ROWS), COLS) // COLS), ROWS)
    rows = round_up(share, ROWS)
    cols = round_up(modes * rows, COLS)
    scale = (1.0 * pairs * nrow * kdev) ** (-0.5)

    flat = jnp.pad(coef_shift.reshape(nq, share, lower * ncond * kdev), ((0, 0), (0, rows - share), (0, 0)))
    zero = jnp.pad(coef_zero.reshape(held, kept, depth), ((0, 0), (0, kept_pad - kept), (0, 0)))
    zero = zero.reshape(held * kept_pad, depth)

    part = lax.dynamic_slice_in_dim(partner, half * groups, groups, axis=0)
    owner = (part // kdev).reshape(groups, nrow, kdev)
    within = (part % kdev).reshape(groups, nrow, kdev)
    ids = jnp.arange(kdev, dtype=jnp.int32)
    slots = jnp.arange(cap, dtype=jnp.int32)
    tri = (ids[:, None] <= ids[None, :]).astype(jnp.bfloat16)

    def ranked(flags):
        counts = jnp.einsum("qdk,kl->qdl", flags.astype(jnp.bfloat16), tri, preferred_element_type=jnp.float32)
        return flags[..., None] & (counts.astype(jnp.int32)[..., None] - 1 == slots)

    chosen = ranked(owner == me).astype(jnp.bfloat16)
    places = (within[..., None] == ids).astype(jnp.bfloat16)
    select = jnp.einsum("qdkx,qdkj->qdxj", places, chosen, preferred_element_type=jnp.float32).astype(jnp.bfloat16)
    my_owner = lax.dynamic_index_in_dim(owner, me, axis=1, keepdims=False)
    match = my_owner[:, None, :] == jnp.arange(nrow, dtype=jnp.int32)[None, :, None]
    perm = jnp.swapaxes(ranked(match), 2, 3).astype(jnp.bfloat16)
    couple = lax.dynamic_slice_in_dim(coupling, half * groups, groups, axis=1).astype(jnp.float32)
    couple = couple.reshape(2, groups, modes * ncond * ncond, kdev)
    spread = pltpu.VMEM((groups, modes * ncond * ncond, 8, kdev), jnp.float32)

    macs = groups * (rows * modes * depth * 4 + 2 * nrow * kept_pad * cols * depth)
    hbm, vmem = pl.BlockSpec(memory_space=pl.ANY), pl.BlockSpec(memory_space=pltpu.VMEM)
    hops = pltpu.VMEM((groups, nrow - 1, wire, COLS), jnp.bfloat16)
    parcels = pltpu.VMEM((groups, nrow, rows, pairs * cap), jnp.bfloat16)
    done = pl.pallas_call(
        functools.partial(main_kernel, (modes, nval, ncond, lower, groups, kept_pad, share, nrow, nexc, scale)),
        out_shape=jax.ShapeDtypeStruct((groups, modes, kept_pad, share), jnp.float32),
        in_specs=[hbm, hbm, vmem, vmem, vmem, vmem],
        out_specs=vmem,
        scratch_shapes=[
            pltpu.VMEM((groups, nrow, ncond * kdev, ncond * cap), jnp.bfloat16),
            pltpu.VMEM((groups, nrow, ncond * cap, ncond * kdev), jnp.bfloat16),
            spread,
            spread,
            pltpu.VMEM((nrow * kept_pad, depth), jnp.bfloat16),
            pltpu.VMEM((nband, groups, rows, lower * ncond * kdev), jnp.bfloat16),
            parcels,
            parcels,
            pltpu.VMEM((rows, depth), jnp.bfloat16),
            pltpu.VMEM((cols, depth), jnp.bfloat16),
            pltpu.VMEM((groups, nrow, wire, COLS), jnp.float32),
            hops,
            hops,
            hops,
            hops,
            pltpu.SemaphoreType.DMA((2,)),
            pltpu.SemaphoreType.DMA((2,)),
            pltpu.SemaphoreType.DMA((nexc,)),
            pltpu.SemaphoreType.DMA((nexc,)),
        ]
        + [pltpu.SemaphoreType.DMA((groups, nrow))] * 6,
        compiler_params=pltpu.CompilerParams(vmem_limit_bytes=LIMIT, collective_id=0, has_side_effects=True),
        cost_estimate=pl.CostEstimate(flops=2 * macs, bytes_accessed=16 * 2**20, transcendentals=0),
        name="coupling",
    )(zero, flat, select, perm, couple[0], couple[1])
    return jnp.transpose(done[:, :, :kept], (2, 0, 1, 3))


def solution(mesh):
    placed = (
        P(("grp", "exc"), None, None, "krow"),
        P(None, ("grp", "exc"), "band", None, "krow"),
        P(None, "grp", None, None, None, "krow"),
        P(),
    )
    return jax.shard_map(
        local,
        mesh=mesh,
        in_specs=placed,
        out_specs=P(("grp", "krow"), "band", None, "exc"),
        check_vma=False,
    )
```

```python
import functools

import jax
import jax.numpy as jnp
from jax import lax
from jax.experimental import pallas as pl
from jax.experimental.pallas import tpu as pltpu
from jax.sharding import PartitionSpec as P

PEERS = 4
ROWS = 16
LANES = 128
COLS = 384
LIMIT = 56 * 2**20
MESH = pl.DeviceIdType.MESH


def round_up(n, unit):
    return (n + unit - 1) // unit * unit


def build_table(x_ref, c_ref, y_ref, d_ref, table, modes, nval, ncond, lower):
    rows = y_ref.shape[1]

    def chunk(r, carry):
        at = pl.multiple_of(r * ROWS, ROWS)

        def slab(ref, g):
            piece = ref[pl.ds(at, ROWS), g * LANES : (g + 1) * LANES]
            return piece.astype(jnp.float32).reshape(ROWS // 8, 8, LANES)

        for v in range(nval):
            own = [w for w in range(nval) if (w // lower == v // lower) == (x_ref is not None)]
            if x_ref is not None:
                shifted = [slab(x_ref, v * ncond + a) for a in range(ncond)]
            for c in range(ncond):
                held = [slab(y_ref.at[w // lower], w % lower * ncond + c) for w in own]
                for m in range(modes):
                    total = None
                    for w, one in zip(own, held):
                        term = one * d_ref[(m * nval + v) * nval + w][None]
                        total = term if total is None else total + term
                    if x_ref is not None:
                        elec = None
                        for a in range(ncond):
                            term = shifted[a] * c_ref[(m * ncond + a) * ncond + c][None]
                            elec = term if elec is None else elec + term
                        total = elec - total
                    g = v * ncond + c
                    table[pl.ds(m * rows + at, ROWS), g * LANES : (g + 1) * LANES] = total.reshape(
                        ROWS, LANES
                    ).astype(jnp.bfloat16)
        return carry

    lax.fori_loop(0, rows // ROWS, chunk, 0)
    used = modes * rows
    if used < table.shape[0]:
        table[used:, :] = jnp.zeros((table.shape[0] - used, table.shape[1]), jnp.bfloat16)


def contract(z_ref, table, write):
    def cols(j, carry):
        at = pl.multiple_of(j * COLS, COLS)
        write(
            at,
            lax.dot_general(
                z_ref[...],
                table[pl.ds(at, COLS), :],
                (((1,), (1,)), ((), ())),
                preferred_element_type=jnp.float32,
            ),
        )
        return carry

    lax.fori_loop(0, table.shape[0] // COLS, cols, 0)


def main_kernel(
    dims, zero_ref, flat_ref, sel_small, perm_small, c_small, d_small, out_ref,
    sel_ref, perm_ref, c_ref, d_ref, zbuf, full, outgo, inc, x_ref, table, part, up_out, up_in, down_out, down_in,
    local_sem, band_sem, exc_send, exc_recv, go_send, go_recv, up_send, up_recv, down_send, down_recv,
):
    modes, nval, ncond, lower, groups, kept_pad, share, nrow, nexc, scale = dims
    me, exc, half = lax.axis_index("krow"), lax.axis_index("exc"), lax.axis_index("band")
    width, wide = sel_ref.shape[2:]
    zrows = zero_ref.shape[0]
    last = nrow - 1

    barrier = pltpu.get_barrier_semaphore()
    for s in range(1, nrow):
        pl.semaphore_signal(barrier, inc=1, device_id={"krow": lax.rem(me + s, nrow)}, device_id_type=MESH)
    for s in range(1, nexc):
        pl.semaphore_signal(barrier, inc=1, device_id={"exc": lax.rem(exc + s, nexc)}, device_id_type=MESH)
    pl.semaphore_signal(barrier, inc=1, device_id={"band": 1 - half}, device_id_type=MESH)
    pl.semaphore_wait(barrier, nrow - 1 + nexc - 1 + 1)

    own_full = pltpu.make_async_copy(flat_ref.at[pl.ds(half * groups, groups)], full.at[half], local_sem.at[0])
    band_copy = pltpu.make_async_remote_copy(
        src_ref=flat_ref.at[pl.ds((1 - half) * groups, groups)],
        dst_ref=full.at[half],
        send_sem=band_sem.at[0],
        recv_sem=band_sem.at[1],
        device_id={"band": 1 - half},
        device_id_type=MESH,
    )
    band_copy.start()
    own_full.start()
    place = pl.ds(pl.multiple_of(exc * zrows, 16), zrows)
    own_zero = pltpu.make_async_copy(zero_ref, zbuf.at[place], local_sem.at[1])
    own_zero.start()
    zero_copies = [
        pltpu.make_async_remote_copy(
            src_ref=zero_ref,
            dst_ref=zbuf.at[place],
            send_sem=exc_send.at[s],
            recv_sem=exc_recv.at[s],
            device_id={"exc": lax.rem(exc + s, nexc)},
            device_id_type=MESH,
        )
        for s in range(1, nexc)
    ]
    for copy in zero_copies:
        copy.start()
    sel_ref[...] = jnp.zeros(sel_ref.shape, sel_ref.dtype)
    perm_ref[...] = jnp.zeros(perm_ref.shape, perm_ref.dtype)
    tall, thin = sel_small.shape[2:]
    for g in range(groups):
        for d in range(nrow):
            for c in range(ncond):
                long, short = slice(c * tall, (c + 1) * tall), slice(c * thin, (c + 1) * thin)
                sel_ref[g, d, long, short] = sel_small[g, d]
                perm_ref[g, d, short, long] = perm_small[g, d]

        def spread(i, carry, g=g):
            c_ref[g, i] = jnp.broadcast_to(c_small[g, pl.ds(i, 1), :], c_ref.shape[2:])
            d_ref[g, i] = jnp.broadcast_to(d_small[g, pl.ds(i, 1), :], d_ref.shape[2:])
            return carry

        lax.fori_loop(0, c_small.shape[1], spread, 0)
    chunks = table.shape[0] // COLS
    used = chunks * kept_pad
    if used < part.shape[2]:
        part[:, :, used:, :] = jnp.zeros(part.shape[:2] + (part.shape[2] - used, COLS), jnp.float32)
    own_full.wait()
    band_copy.wait()

    go_copies = []
    for g in range(groups):
        row = [None]
        for s in list(range(1, nrow)) + [0]:
            dest = lax.rem(me + s, nrow)
            target = outgo if s else inc
            for v in range(nval):
                at = v % lower * width
                got = jnp.dot(
                    full[v // lower, g, :, at : at + width], sel_ref[g, dest], preferred_element_type=jnp.float32
                )
                target[g, s, :, v * wide : (v + 1) * wide] = got.astype(jnp.bfloat16)
            if s:
                copy = pltpu.make_async_remote_copy(
                    src_ref=outgo.at[g, s],
                    dst_ref=inc.at[g, s],
                    send_sem=go_send.at[g, s],
                    recv_sem=go_recv.at[g, s],
                    device_id={"krow": dest},
                    device_id_type=MESH,
                )
                copy.start()
                row.append(copy)
        go_copies.append(row)

    def contract(write):
        def cols(j, carry):
            at = pl.multiple_of(j * COLS, COLS)
            got = lax.dot_general(
                zbuf[...], table[pl.ds(at, COLS), :], (((1,), (1,)), ((), ())), preferred_element_type=jnp.float32
            )
            for d in range(nrow):
                write(d, pl.ds(pl.multiple_of(j * kept_pad, 8), kept_pad), got[d * kept_pad : (d + 1) * kept_pad])
            return carry

        lax.fori_loop(0, chunks, cols, 0)

    for g in range(groups):
        build_table(None, None, full.at[:, g], d_ref.at[g], table, modes, nval, ncond, lower)
        if g == 0:
            own_zero.wait()
            for copy in zero_copies:
                copy.wait()

        def first_part(d, at, got, g=g):
            part[g, d, at, :] = -got

        contract(first_part)

    def neighbour(g, t, out, into, send, recv, device):
        return pltpu.make_async_remote_copy(
            src_ref=out.at[g, t],
            dst_ref=into.at[g, t],
            send_sem=send.at[g, t],
            recv_sem=recv.at[g, t],
            device_id={"krow": device},
            device_id_type=MESH,
        )

    def flow(up):
        if up:
            return me, lambda t: me + nrow - t, lambda g, t: neighbour(
                g, t - 1, up_out, up_in, up_send, up_recv, lax.rem(me + 1, nrow)
            )
        return last - me, lambda t: me - nrow + t, lambda g, t: neighbour(
            g, t - 1, down_out, down_in, down_send, down_recv, lax.rem(me + last, nrow)
        )

    def step(g, t):
        for up in (True, False):
            pos, block, copy = flow(up)
            out, into = (up_out, up_in) if up else (down_out, down_in)

            def mine(block=block):
                return part[g, jnp.clip(block(t), 0, last)]

            @pl.when((pos >= 1) & (pos <= t - 1))
            def _(out=out, into=into, copy=copy, mine=mine):
                copy(g, t - 1).wait_recv()
                out[g, t - 1] = (mine() + into[g, t - 2].astype(jnp.float32)).astype(jnp.bfloat16)
                copy(g, t).start()

    def ends(g):
        for t in range(1, nrow):
            for up in (True, False):
                pos, block, copy = flow(up)
                out = up_out if up else down_out

                @pl.when(pos == 0)
                def _(out=out, block=block, copy=copy):
                    out[g, t - 1] = part[g, jnp.clip(block(t), 0, last)].astype(jnp.bfloat16)
                    copy(g, t).start()

    def finish(g):
        for up in (True, False):
            pos, _, copy = flow(up)
            into = up_in if up else down_in

            @pl.when(pos >= 1)
            def _(into=into, copy=copy):
                copy(g, last).wait_recv()
                part[g, me] = part[g, me] + into[g, last - 1].astype(jnp.float32)

        total = jnp.concatenate(
            [part[g, me, j * kept_pad : (j + 1) * kept_pad, :] for j in range(chunks)], axis=1
        )
        rows = x_ref.shape[0]
        for m in range(modes):
            out_ref[g, m] = total[:, m * rows : m * rows + share] * scale

    def elec(g, between):
        for copy in go_copies[g][1:]:
            copy.wait_recv()
        for v in range(nval):
            got = jnp.zeros((x_ref.shape[0], width), jnp.float32)
            for s in range(nrow):
                owner = lax.rem(me + nrow - s, nrow)
                got = got + jnp.dot(
                    inc[g, s, :, v * wide : (v + 1) * wide], perm_ref[g, owner], preferred_element_type=jnp.float32
                )
            x_ref[:, v * width : (v + 1) * width] = got.astype(jnp.bfloat16)
        build_table(x_ref, c_ref.at[g], full.at[:, g], d_ref.at[g], table, modes, nval, ncond, lower)
        between()

        def add_part(d, at, got):
            part[g, d, at, :] = part[g, d, at, :] + got

        contract(add_part)

    for g in range(groups):

        def between(g=g):
            if g > 0 and nrow > 2:
                step(g - 1, 2)

        elec(g, between)
        ends(g)
        if g > 0:
            for t in range(3, nrow):
                step(g - 1, t)
            if g < groups - 1:
                finish(g - 1)
    for t in range(2, nrow):
        step(groups - 1, t)
        if t == 2 and groups > 1:
            finish(groups - 2)
    if nrow == 2 and groups > 1:
        finish(groups - 2)
    finish(groups - 1)

    for g in range(groups):
        for copy in go_copies[g][1:]:
            copy.wait_send()
        for t in range(1, nrow):
            for up in (True, False):
                pos, _, copy = flow(up)

                @pl.when(pos <= t - 1)
                def _(copy=copy):
                    copy(g, t).wait_send()


def local(coef_zero, coef_shift, coupling, partner):
    nrow = lax.axis_size("krow")
    me = lax.axis_index("krow")
    nband = lax.axis_size("band")
    half = lax.axis_index("band")
    nexc = lax.axis_size("exc")
    mine, nval, ncond, kdev = coef_zero.shape
    nq, share, lower = coef_shift.shape[:3]
    modes = coupling.shape[2]
    cap = kdev // PEERS
    pairs = nval * ncond
    depth = pairs * kdev
    groups = nq // nband
    kept = mine * nexc // nrow
    held = mine // kept
    kept_pad = round_up(kept, 8)
    wire = round_up(kept_pad * (round_up(modes * round_up(share, ROWS), COLS) // COLS), ROWS)
    rows = round_up(share, ROWS)
    cols = round_up(modes * rows, COLS)
    scale = (1.0 * pairs * nrow * kdev) ** (-0.5)

    flat = jnp.pad(coef_shift.reshape(nq, share, lower * ncond * kdev), ((0, 0), (0, rows - share), (0, 0)))
    zero = jnp.pad(coef_zero.reshape(held, kept, depth), ((0, 0), (0, kept_pad - kept), (0, 0)))
    zero = zero.reshape(held * kept_pad, depth)

    part = lax.dynamic_slice_in_dim(partner, half * groups, groups, axis=0)
    owner = (part // kdev).reshape(groups, nrow, kdev)
    within = (part % kdev).reshape(groups, nrow, kdev)
    ids = jnp.arange(kdev, dtype=jnp.int32)
    slots = jnp.arange(cap, dtype=jnp.int32)
    tri = (ids[:, None] <= ids[None, :]).astype(jnp.bfloat16)

    def ranked(flags):
        counts = jnp.einsum("qdk,kl->qdl", flags.astype(jnp.bfloat16), tri, preferred_element_type=jnp.float32)
        return flags[..., None] & (counts.astype(jnp.int32)[..., None] - 1 == slots)

    chosen = ranked(owner == me).astype(jnp.bfloat16)
    places = (within[..., None] == ids).astype(jnp.bfloat16)
    select = jnp.einsum("qdkx,qdkj->qdxj", places, chosen, preferred_element_type=jnp.float32).astype(jnp.bfloat16)
    my_owner = lax.dynamic_index_in_dim(owner, me, axis=1, keepdims=False)
    match = my_owner[:, None, :] == jnp.arange(nrow, dtype=jnp.int32)[None, :, None]
    perm = jnp.swapaxes(ranked(match), 2, 3).astype(jnp.bfloat16)
    couple = lax.dynamic_slice_in_dim(coupling, half * groups, groups, axis=1).astype(jnp.float32)
    couple = couple.reshape(2, groups, modes * ncond * ncond, kdev)
    spread = pltpu.VMEM((groups, modes * ncond * ncond, 8, kdev), jnp.float32)

    macs = groups * (rows * modes * depth * 4 + 2 * nrow * kept_pad * cols * depth)
    hbm, vmem = pl.BlockSpec(memory_space=pl.ANY), pl.BlockSpec(memory_space=pltpu.VMEM)
    hops = pltpu.VMEM((groups, nrow - 1, wire, COLS), jnp.bfloat16)
    parcels = pltpu.VMEM((groups, nrow, rows, pairs * cap), jnp.bfloat16)
    done = pl.pallas_call(
        functools.partial(main_kernel, (modes, nval, ncond, lower, groups, kept_pad, share, nrow, nexc, scale)),
        out_shape=jax.ShapeDtypeStruct((groups, modes, kept_pad, share), jnp.float32),
        in_specs=[hbm, hbm, vmem, vmem, vmem, vmem],
        out_specs=vmem,
        scratch_shapes=[
            pltpu.VMEM((groups, nrow, ncond * kdev, ncond * cap), jnp.bfloat16),
            pltpu.VMEM((groups, nrow, ncond * cap, ncond * kdev), jnp.bfloat16),
            spread,
            spread,
            pltpu.VMEM((nrow * kept_pad, depth), jnp.bfloat16),
            pltpu.VMEM((nband, groups, rows, lower * ncond * kdev), jnp.bfloat16),
            parcels,
            parcels,
            pltpu.VMEM((rows, depth), jnp.bfloat16),
            pltpu.VMEM((cols, depth), jnp.bfloat16),
            pltpu.VMEM((groups, nrow, wire, COLS), jnp.float32),
            hops,
            hops,
            hops,
            hops,
            pltpu.SemaphoreType.DMA((2,)),
            pltpu.SemaphoreType.DMA((2,)),
            pltpu.SemaphoreType.DMA((nexc,)),
            pltpu.SemaphoreType.DMA((nexc,)),
        ]
        + [pltpu.SemaphoreType.DMA((groups, nrow))] * 6,
        compiler_params=pltpu.CompilerParams(vmem_limit_bytes=LIMIT, collective_id=0, has_side_effects=True),
        cost_estimate=pl.CostEstimate(flops=2 * macs, bytes_accessed=16 * 2**20, transcendentals=0),
        name="coupling",
    )(zero, flat, select, perm, couple[0], couple[1])
    return jnp.transpose(done[:, :, :kept], (2, 0, 1, 3))


def solution(mesh):
    placed = (
        P(("grp", "exc"), None, None, "krow"),
        P(None, ("grp", "exc"), "band", None, "krow"),
        P(None, "grp", None, None, None, "krow"),
        P(),
    )
    return jax.shard_map(
        local,
        mesh=mesh,
        in_specs=placed,
        out_specs=P(("grp", "krow"), "band", None, "exc"),
        check_vma=False,
    )
```
